32 devices in a mesh: dp: 4 (over z), ctx: 8 (over y, x, core).
Axes of the slice: x: 2, y: 2, z: 4, core: 2. Of those that a mesh axis runs over, the one named last changes fastest.
Arguments:
- query_in: bfloat16 [4, 1024, 2048], P('dp', 'ctx'), may hold values from -6 to 6
- key_in: bfloat16 [4, 1024, 2048], P('dp', 'ctx'), may hold values from -6 to 6
- value_in: bfloat16 [4, 1024, 2048], P('dp', 'ctx'), may hold values from -6 to 6
- out_grad: bfloat16 [4, 1024, 2048], P('dp', 'ctx'), may hold values from -6 to 6
- log_decay: bfloat16 [4, 1024, 32], P('dp', 'ctx'), may hold values from -2 to 0, as said below
- doc_ids: int32 [4, 8], P('dp'), may hold values from 0 to 3, never falling along the last dimension, each value on 1 to 4 neighbouring positions
- norm_gain: float32 [2048], replicated, may hold values from 0.1 to 1.9
Outputs:
- query_grad: bfloat16 [4, 1024, 2048], P('dp', 'ctx')
- key_grad: bfloat16 [4, 1024, 2048], P('dp', 'ctx')
- value_grad: bfloat16 [4, 1024, 2048], P('dp', 'ctx')
- gain_grad: float32 [2048], replicated
The draws below stay inside these ranges and needn't reach their ends.
Inputs may be any that keep to these rules, and one draw needn't show every extreme that they name: log_decay is never positive. Within a sequence doc_ids never fall; each of the 4 documents covers 1 to half of 8 blocks, and one covers exactly half of 8.
All inputs are finite; a program needn't handle non-finite values.
Results may differ from the reference program's by a relative error of at most 0.0061.
Values may be sent and summed in bfloat16 or wider, within the bound.
A program may use at most 192 MiB of HBM per device.

```python
import math
import jax
import jax.numpy as jnp
import numpy as np
from jax import lax

HEAD_TOTAL = 32
DH = 64
BLOCK = 128
TOK_DEV = 128
BATCH_ROWS = 4
SEQ = 1024
NBLK = 8


def head_pattern(key, slow_percent):
    key = jax.random.fold_in(key, 101)
    subkeys = jax.random.split(key, 3)
    slow_heads = jax.random.randint(subkeys[0], (BATCH_ROWS, 1, HEAD_TOTAL), 0, 100) < slow_percent
    row_keys = jax.random.split(subkeys[1], BATCH_ROWS)
    head_orders = jax.vmap(lambda row_key: jax.random.permutation(row_key, HEAD_TOTAL))(row_keys)
    steep_heads = (head_orders < 2)[:, None, :]
    slow_heads = slow_heads & jnp.logical_not(steep_heads)
    loudness = jnp.exp(jax.random.uniform(subkeys[2], (BATCH_ROWS, NBLK, 1, 1, 1), minval=math.log(0.06), maxval=0.0))
    return (slow_heads, steep_heads, loudness)


def scaled_rows(base_noise, slow_heads, loudness):
    amplitude = jnp.where(slow_heads, 0.25, 1.0).reshape(BATCH_ROWS, 1, 1, HEAD_TOTAL, 1)
    shaped = base_noise * loudness * amplitude
    return shaped.reshape(BATCH_ROWS, SEQ, HEAD_TOTAL * DH).astype(jnp.float32).astype(jnp.bfloat16)


def draw_key_in(key, part):
    slow_percent = 50
    slow_heads, steep_heads, loudness = head_pattern(key, slow_percent)
    key = jax.random.fold_in(key, 11)
    base_noise = jnp.clip(jax.random.normal(key, (BATCH_ROWS, NBLK, BLOCK, HEAD_TOTAL, DH)), -6.0, 6.0)
    return scaled_rows(base_noise, slow_heads, loudness)


def draw_value_in(key, part):
    slow_percent = 50
    slow_heads, steep_heads, loudness = head_pattern(key, slow_percent)
    key = jax.random.fold_in(key, 12)
    base_noise = jnp.clip(jax.random.normal(key, (BATCH_ROWS, NBLK, BLOCK, HEAD_TOTAL, DH)), -6.0, 6.0)
    return scaled_rows(base_noise, slow_heads, loudness)


def draw_log_decay(key, part):
    slow_percent = 50
    slow_heads, steep_heads, loudness = head_pattern(key, slow_percent)
    key = jax.random.fold_in(key, 13)
    subkeys = jax.random.split(key, 7)
    coarse_estimate = jnp.exp(jax.random.uniform(subkeys[4], (BATCH_ROWS, SEQ, HEAD_TOTAL), minval=-0.4, maxval=0.4))
    slow_rate = jax.random.uniform(subkeys[1], (BATCH_ROWS, 1, HEAD_TOTAL), minval=0.1, maxval=0.4) / SEQ
    fast_rate = jnp.exp(jax.random.uniform(subkeys[2], (BATCH_ROWS, 1, HEAD_TOTAL), minval=math.log(1.0 / 50.0), maxval=math.log(1.0 / 30.0)))
    baseline_rate = jnp.where(slow_heads, slow_rate, fast_rate)
    shard_multiplier = jnp.exp(jax.random.uniform(subkeys[3], (BATCH_ROWS, SEQ // TOK_DEV, 1, HEAD_TOTAL), minval=-0.7, maxval=0.7))
    shard_multiplier = jnp.broadcast_to(shard_multiplier, (BATCH_ROWS, SEQ // TOK_DEV, TOK_DEV, HEAD_TOTAL)).reshape(BATCH_ROWS, SEQ, HEAD_TOTAL)
    spots = jax.random.randint(subkeys[5], (BATCH_ROWS, 2, 1), 0, SEQ)
    reset_hits = jnp.any(jnp.arange(SEQ)[None, None, :] == spots, axis=1)
    spike_logarithm = jnp.log(jax.random.uniform(subkeys[6], (BATCH_ROWS, 1, HEAD_TOTAL), minval=0.5, maxval=0.8))
    spike_amount = jnp.where(reset_hits[:, :, None], spike_logarithm, 0.0)
    value_rows = -(baseline_rate * shard_multiplier * coarse_estimate) + spike_amount
    steep_rows = -jax.random.uniform(subkeys[0], (BATCH_ROWS, SEQ, HEAD_TOTAL), minval=1.5, maxval=2.0)
    value_rows = jnp.where(steep_heads, steep_rows, value_rows)
    return value_rows.astype(jnp.float32).astype(jnp.bfloat16)


def shard_levels(own_key, dims, shards, smallest, high):
    level = 1.0
    for axis_at, blocks in shards:
        heights = jax.random.uniform(jax.random.fold_in(jax.random.fold_in(own_key, 6), axis_at), (blocks,), jnp.float32, smallest / len(shards), high / len(shards))
        level = level * jnp.repeat(jnp.exp(heights), dims[axis_at] // blocks).reshape((-1,) + (1,) * (len(dims) - 1 - axis_at))
    return level


def split_up(number_of, total, most, slope):
    portions = [(1 << 20) // math.isqrt(rank ** slope) + 1 for rank in range(2, number_of + 1)]
    spare, holding = total - most - (number_of - 1), [1] * (number_of - 1)
    while spare > 0:
        candidates = [i for i in range(number_of - 1) if holding[i] < most]
        pool, left = sum([portions[i] for i in candidates]), spare
        for i in candidates:
            extra = min(most - holding[i], max(1, left * portions[i] // pool), spare)
            holding[i] = holding[i] + extra
            spare = spare - extra
    return np.array([most] + holding)


def ragged(own_key, count, total, reach, skew):
    if count == 2:
        one = jax.random.randint(own_key, (), max(1, total - reach), min(reach, total - 1) + 1)
        return jnp.stack([one, total - one])
    tallies = jnp.asarray(split_up(count, total, reach, skew), jnp.int32)
    twos = (count - 1) // 2
    giver, receiver = tallies[1:1 + 2 * twos:2], tallies[2:2 + 2 * twos:2]
    slack = jnp.minimum(giver - 1, reach - receiver)
    shifted = jax.random.randint(jax.random.fold_in(own_key, 1), (twos,), 0, 1 << 20) % (slack + 1)
    tallies = tallies.at[1:1 + 2 * twos:2].set(giver - shifted).at[2:2 + 2 * twos:2].set(receiver + shifted)
    return tallies[jax.random.permutation(jax.random.fold_in(own_key, 2), count)]


def normal_values(stream_key, extent, scale, most, cuts=(), held_as=jnp.bfloat16):
    entries = scale * jax.random.normal(stream_key, extent, jnp.float32)
    if cuts:
        entries = entries * shard_levels(stream_key, extent, cuts, -0.22, 0.18)
    return jnp.clip(entries, -most, most).astype(held_as)


def setup_inputs(seed: int = 0) -> dict:
    splits = jax.random.split(jax.random.key(seed), 8)
    return {
        "query_in": normal_values(splits[0], (BATCH_ROWS, SEQ, HEAD_TOTAL * DH), 1.0, 6.0, ((0, 4), (1, 8))),
        "key_in": draw_key_in(jax.random.fold_in(splits[7], 71), 0),
        "value_in": draw_value_in(jax.random.fold_in(splits[7], 71), 0),
        "out_grad": normal_values(splits[3], (BATCH_ROWS, SEQ, HEAD_TOTAL * DH), 1.0, 6.0, ((0, 4), (1, 8))),
        "log_decay": draw_log_decay(jax.random.fold_in(splits[7], 71), 0),
        "doc_ids": jax.vmap(lambda own: jnp.searchsorted(jnp.cumsum(ragged(own, 4, NBLK, NBLK // 2, 0)), jnp.arange(NBLK), side="right"))(jax.random.split(splits[5], BATCH_ROWS)).reshape((BATCH_ROWS, NBLK)).astype(jnp.int32),
        "norm_gain": jnp.clip(1.0 + 0.18 * jax.random.normal(splits[6], (HEAD_TOTAL * DH,), jnp.float32), 0.1, 1.9),
    }


HIGHEST_PRECISION = lax.Precision.HIGHEST
EPSILON = 1e-05

def block_tables(log_rate, start_flag):
    within = jnp.cumsum(log_rate, axis=0)
    block_total = within[-1]
    keep_state = 1.0 - start_flag
    head_weight = jnp.exp(within) * keep_state
    tail_weight = jnp.exp(block_total[None, :] - within)
    within_heads = jnp.transpose(within)
    log_gaps = within_heads[:, :, None] - within_heads[:, None, :]
    causal = jnp.arange(BLOCK)[:, None] >= jnp.arange(BLOCK)[None, :]
    intra_weight = jnp.where(causal[None], jnp.exp(jnp.minimum(log_gaps, 0.0)), 0.0)
    carry_decay = jnp.exp(block_total) * keep_state
    return (intra_weight, head_weight, tail_weight, carry_decay)

def product(form, left, right):
    return jnp.einsum(form, left.astype(jnp.float32), right.astype(jnp.float32), precision=HIGHEST_PRECISION)

def sequence_pass(query_seq, key_seq, value_seq, grad_seq, decay_seq, doc_seq, norm_gain):
    query_blocks = query_seq.reshape(NBLK, BLOCK, HEAD_TOTAL, DH)
    key_blocks = key_seq.reshape(NBLK, BLOCK, HEAD_TOTAL, DH)
    value_blocks = value_seq.reshape(NBLK, BLOCK, HEAD_TOTAL, DH)
    decay_blocks = decay_seq.astype(jnp.float32).reshape(NBLK, BLOCK, HEAD_TOTAL)
    starts = jnp.concatenate([jnp.ones((1,), jnp.float32), (doc_seq[1:] != doc_seq[:-1]).astype(jnp.float32)])

    def forward_step(state, items):
        query_blk, key_blk, value_blk, log_rate, start_flag = items
        intra_weight, head_weight, tail_weight, carry_decay = block_tables(log_rate, start_flag)
        block_probs = (product('thd,shd->hts', query_blk, key_blk) * intra_weight).astype(jnp.bfloat16)
        local_part = product('hts,shd->thd', block_probs, value_blk)
        weighted = (query_blk.astype(jnp.float32) * head_weight[:, :, None]).astype(jnp.bfloat16)
        carried = product('thd,hde->the', weighted, state.astype(jnp.bfloat16))
        keyed = (key_blk.astype(jnp.float32) * tail_weight[:, :, None]).astype(jnp.bfloat16)
        new_state = carry_decay[:, None, None] * state + product('shd,she->hde', keyed, value_blk)
        return (new_state, (local_part + carried, state))
    zero_state = jnp.zeros((HEAD_TOTAL, DH, DH), jnp.float32)
    _, (attn_blocks, states_before) = lax.scan(forward_step, zero_state, (query_blocks, key_blocks, value_blocks, decay_blocks, starts))
    attn_flat = attn_blocks.reshape(SEQ, HEAD_TOTAL * DH)
    grad_flat = grad_seq.astype(jnp.float32)
    scaled = norm_gain[None, :] * grad_flat
    count = HEAD_TOTAL * DH
    inv_rms = lax.rsqrt(lax.optimization_barrier(jnp.sum(attn_flat * attn_flat, axis=1)) / count + EPSILON)
    cross = lax.optimization_barrier(jnp.sum(attn_flat * scaled, axis=1))
    grad_input = inv_rms[:, None] * scaled - (inv_rms * inv_rms * inv_rms * cross / count)[:, None] * attn_flat
    grad_input = grad_input.astype(jnp.bfloat16)
    gain_part = lax.optimization_barrier(jnp.sum(grad_flat * attn_flat * inv_rms[:, None], axis=0))
    grad_blocks = grad_input.reshape(NBLK, BLOCK, HEAD_TOTAL, DH)

    def backward_step(state, items):
        query_blk, key_blk, value_blk, grad_blk, log_rate, start_flag, before = items
        intra_weight, head_weight, tail_weight, carry_decay = block_tables(log_rate, start_flag)
        block_probs = (product('thd,shd->hts', query_blk, key_blk) * intra_weight).astype(jnp.bfloat16)
        grad_scores = (product('thd,shd->hts', grad_blk, value_blk) * intra_weight).astype(jnp.bfloat16)
        weighted_grad = (grad_blk.astype(jnp.float32) * head_weight[:, :, None]).astype(jnp.bfloat16)
        state_low = state.astype(jnp.bfloat16)
        grad_query = product('hts,shd->thd', grad_scores, key_blk) + product('the,hde->thd', weighted_grad, before.astype(jnp.bfloat16))
        grad_key = product('hts,thd->shd', grad_scores, query_blk) + tail_weight[:, :, None] * product('she,hde->shd', value_blk, state_low)
        grad_value = product('hts,the->she', block_probs, grad_blk) + tail_weight[:, :, None] * product('shd,hde->she', key_blk, state_low)
        queried = (query_blk.astype(jnp.float32) * head_weight[:, :, None]).astype(jnp.bfloat16)
        new_state = carry_decay[:, None, None] * state + product('thd,the->hde', queried, grad_blk)
        return (new_state, (grad_query.astype(jnp.bfloat16), grad_key.astype(jnp.bfloat16), grad_value.astype(jnp.bfloat16)))
    _, (grad_query, grad_key, grad_value) = lax.scan(backward_step, zero_state, (query_blocks, key_blocks, value_blocks, grad_blocks, decay_blocks, starts, states_before), reverse=True)
    return (grad_query.reshape(SEQ, HEAD_TOTAL * DH), grad_key.reshape(SEQ, HEAD_TOTAL * DH), grad_value.reshape(SEQ, HEAD_TOTAL * DH), gain_part)

def reference(query_in, key_in, value_in, out_grad, log_decay, doc_ids, norm_gain):

    def one_sequence(items):
        query_seq, key_seq, value_seq, grad_seq, decay_seq, doc_seq = items
        return sequence_pass(query_seq, key_seq, value_seq, grad_seq, decay_seq, doc_seq, norm_gain)
    query_grad, key_grad, value_grad, gain_parts = lax.map(one_sequence, (query_in, key_in, value_in, out_grad, log_decay, doc_ids))
    gain_grad = lax.optimization_barrier(jnp.sum(gain_parts, axis=0)) / math.sqrt(BATCH_ROWS * SEQ)
    return (query_grad, key_grad, value_grad, gain_grad)
```

```python
import functools
import math

import jax
import jax.numpy as jnp
from jax import lax
from jax.experimental import pallas as pl
from jax.experimental.pallas import tpu as pltpu
from jax.sharding import PartitionSpec as P

EPSILON = 1e-05
MESH = pl.DeviceIdType.MESH
UNROLL = 4
F32 = jnp.float32
BF16 = jnp.bfloat16


def dot(left, right, left_dim, right_dim):
    return lax.dot_general(
        left, right, (((left_dim,), (right_dim,)), ((), ())), preferred_element_type=F32
    )


def kernel(
    ctx_count, dp_count, tokens,
    q_ref, k_ref, v_ref, g_ref, decay_ref, doc_ref, gain_ref,
    dq_ref, dk_ref, dv_ref, gain_out_ref,
    rows_s, weight_s, head_s, tail_s, probs_s, attn_s, grad_s, qw_s, dk_s, dv_s,
    carry_all, term_out, term_in, state_out, state_in,
    back_term_out, back_term_in, back_out, back_in,
    gain_all, gain_mid, gain_dp,
    send_sem, recv_sem, gain_send_sem, gain_recv_sem,
):
    length, width = q_ref.shape
    lanes = 128
    half = lanes // 2
    pairs = width // lanes
    chunk = pairs * half // ctx_count
    me = lax.axis_index("ctx")
    row_me = lax.axis_index("dp")

    barrier = pltpu.get_barrier_semaphore()
    for j in range(1, ctx_count):
        other = lax.rem(me + j, ctx_count)
        pl.semaphore_signal(barrier, inc=1, device_id={"ctx": other}, device_id_type=MESH)
    for j in range(1, dp_count):
        other = lax.rem(row_me + j, dp_count)
        pl.semaphore_signal(barrier, inc=1, device_id={"dp": other}, device_id_type=MESH)

    left_half = lax.broadcasted_iota(jnp.int32, (1, lanes), 1) < half

    def cols(pair):
        return pl.ds(pl.multiple_of(pair * lanes, lanes), lanes)

    def packed_rows(pair):
        return pl.ds(pl.multiple_of(pair * half, half), half)

    def pick(first, second):
        return jnp.where(left_half, first, second)

    def stacked(block):
        zero = jnp.zeros_like(block)
        return jnp.concatenate([pick(block, zero), pick(zero, block)], axis=0)

    def packed(full, size):
        return pick(full[:size], full[size:])

    def over_pairs(first, last, fn, init=0):
        return lax.fori_loop(first, last, fn, init, unroll=UNROLL)

    step_row = lax.broadcasted_iota(jnp.int32, (length, length), 0)
    step_col = lax.broadcasted_iota(jnp.int32, (length, length), 1)
    upto = jnp.where(step_row <= step_col, 1.0, 0.0).astype(BF16)
    rows_s[...] = dot(decay_ref[...], upto, 0, 0)

    same_doc = doc_ref[0, me] == doc_ref[0, jnp.maximum(me - 1, 0)]
    keep = jnp.where(same_doc, 1.0, 0.0) * jnp.where(me == 0, 0.0, 1.0)

    def column(head):
        row = rows_s[pl.ds(head, 1), :]
        return row, jnp.transpose(jnp.broadcast_to(row, (length, lanes)))

    def terms_step(pair, _):
        _, first = column(2 * pair)
        _, second = column(2 * pair + 1)
        within = pick(first, second)
        total = within[length - 1 :, :]
        tail = jnp.exp(total - within)
        tail_s[:, cols(pair)] = tail
        head_s[:, cols(pair)] = jnp.exp(within) * keep
        carry_all[me, pl.ds(pair, 1), :] = jnp.exp(total) * keep
        keyed = (k_ref[:, cols(pair)].astype(F32) * tail).astype(BF16)
        full = dot(keyed, v_ref[:, cols(pair)], 0, 0)
        term_out[packed_rows(pair), :] = packed(full, half).astype(BF16)
        return 0

    over_pairs(0, pairs, terms_step)
    pl.semaphore_wait(barrier, ctx_count - 1 + dp_count - 1)

    def piece(index):
        return pl.ds(pl.multiple_of(index * chunk, chunk), chunk)

    def to_all(phase, source, target):
        copies = []
        for j in range(1, ctx_count):
            other = lax.rem(me + j, ctx_count)
            copies.append(
                pltpu.make_async_remote_copy(
                    src_ref=source(other),
                    dst_ref=target(),
                    send_sem=send_sem.at[phase, j],
                    recv_sem=recv_sem.at[phase, j],
                    device_id={"ctx": other},
                    device_id_type=MESH,
                )
            )
        for copy in copies:
            copy.start()
        return copies

    def finish(copies):
        for copy in copies:
            copy.wait()

    def combine(term_ref, out_ref, backward):
        per = max(chunk // half, 1)
        size = min(chunk, half)
        running = [jnp.zeros((size, lanes), F32) for _ in range(per)]
        order = range(ctx_count - 1, -1, -1) if backward else range(ctx_count)
        for block in order:
            for i in range(per):
                pair = lax.div(me * chunk, half) + i
                out_ref[block, i * size : (i + 1) * size, :] = running[i].astype(BF16)
                carry = carry_all[block, pl.ds(pair, 1), :]
                running[i] = carry * running[i] + term_ref[
                    block, i * size : (i + 1) * size, :
                ].astype(F32)

    def exchange_terms(phase, out_ref, in_ref):
        in_ref[me] = out_ref[piece(me), :]
        return to_all(phase, lambda other: out_ref.at[piece(other), :], lambda: in_ref.at[me])

    def exchange_states(phase, out_ref, in_ref):
        in_ref[piece(me), :] = out_ref[me]
        return to_all(phase, lambda other: out_ref.at[other], lambda: in_ref.at[piece(me), :])

    carry_copies = to_all(0, lambda other: carry_all.at[me], lambda: carry_all.at[me])
    term_copies = exchange_terms(1, term_out, term_in)

    causal = step_row >= step_col

    def local_step(pair, _):
        weights = []
        for head in (2 * pair, 2 * pair + 1):
            row, col = column(head)
            weights.append(jnp.where(causal, jnp.exp(jnp.minimum(col - row, 0.0)), 0.0))
        weight = jnp.concatenate(weights, axis=1)
        weight_s[pair] = weight
        scores = dot(q_ref[:, cols(pair)], stacked(k_ref[:, cols(pair)]), 1, 1)
        probs = (scores * weight).astype(BF16)
        probs_s[pair] = probs
        attn_s[:, cols(pair)] = dot(probs, stacked(v_ref[:, cols(pair)]), 1, 0)
        qw_s[:, cols(pair)] = (q_ref[:, cols(pair)].astype(F32) * head_s[:, cols(pair)]).astype(BF16)
        return 0

    over_pairs(0, pairs // 2, local_step)
    finish(carry_copies)
    finish(term_copies)
    combine(term_in, state_out, False)
    state_copies = exchange_states(2, state_out, state_in)
    over_pairs(pairs // 2, pairs, local_step)
    finish(state_copies)

    def attend_step(pair, sums):
        square, cross = sums
        carried = dot(qw_s[:, cols(pair)], stacked(state_in[packed_rows(pair), :]), 1, 0)
        attn = attn_s[:, cols(pair)] + carried
        attn_s[:, cols(pair)] = attn
        scaled = gain_ref[:, cols(pair)] * g_ref[:, cols(pair)].astype(F32)
        return square + attn * attn, cross + attn * scaled

    zero = jnp.zeros((length, lanes), F32)
    square, cross = over_pairs(0, pairs, attend_step, (zero, zero))
    inv_rms = lax.rsqrt(jnp.sum(square, axis=1, keepdims=True) / width + EPSILON)
    shift = inv_rms * inv_rms * inv_rms * jnp.sum(cross, axis=1, keepdims=True) / width

    def norm_step(pair, _):
        grad_out = g_ref[:, cols(pair)].astype(F32)
        attn = attn_s[:, cols(pair)]
        grad = inv_rms * (gain_ref[:, cols(pair)] * grad_out) - shift * attn
        grad = grad.astype(BF16)
        grad_s[:, cols(pair)] = grad
        full = dot(qw_s[:, cols(pair)], grad, 0, 0)
        back_term_out[packed_rows(pair), :] = packed(full, half).astype(BF16)
        gain_all[me, :, cols(pair)] = jnp.sum(grad_out * attn * inv_rms, axis=0, keepdims=True)
        return 0

    over_pairs(0, pairs, norm_step)
    back_term_copies = exchange_terms(3, back_term_out, back_term_in)
    gain_copies = to_all(4, lambda other: gain_all.at[me], lambda: gain_all.at[me])

    def grads_step(pair, _):
        grad = grad_s[:, cols(pair)]
        scores = dot(grad, stacked(v_ref[:, cols(pair)]), 1, 1)
        scores = (scores * weight_s[pair]).astype(BF16)
        weighted = (grad.astype(F32) * head_s[:, cols(pair)]).astype(BF16)
        dq = dot(scores, stacked(k_ref[:, cols(pair)]), 1, 0)
        dq = dq + dot(weighted, stacked(state_in[packed_rows(pair), :]), 1, 1)
        dq_ref[:, cols(pair)] = dq.astype(BF16)
        dk_s[:, cols(pair)] = packed(dot(scores, q_ref[:, cols(pair)], 0, 0), length)
        dv_s[:, cols(pair)] = packed(dot(probs_s[pair], grad, 0, 0), length)
        return 0

    over_pairs(0, pairs // 2, grads_step)
    finish(back_term_copies)
    combine(back_term_in, back_out, True)
    back_copies = exchange_states(5, back_out, back_in)
    finish(gain_copies)
    gain_ctx = gain_all[0]
    for block in range(1, ctx_count):
        gain_ctx = gain_ctx + gain_all[block]
    gain_mid[...] = gain_ctx
    dp_copies = []
    for j in range(1, dp_count):
        other = lax.rem(row_me + j, dp_count)
        dp_copies.append(
            pltpu.make_async_remote_copy(
                src_ref=gain_mid,
                dst_ref=gain_dp.at[row_me],
                send_sem=gain_send_sem.at[j],
                recv_sem=gain_recv_sem.at[j],
                device_id={"dp": other},
                device_id_type=MESH,
            )
        )
    for copy in dp_copies:
        copy.start()
    gain_dp[row_me] = gain_ctx
    over_pairs(pairs // 2, pairs, grads_step)
    finish(back_copies)

    def last_step(pair, _):
        back = stacked(back_in[packed_rows(pair), :])
        tail = tail_s[:, cols(pair)]
        dk = dk_s[:, cols(pair)] + tail * dot(v_ref[:, cols(pair)], back, 1, 1)
        dv = dv_s[:, cols(pair)] + tail * dot(k_ref[:, cols(pair)], back, 1, 0)
        dk_ref[:, cols(pair)] = dk.astype(BF16)
        dv_ref[:, cols(pair)] = dv.astype(BF16)
        return 0

    over_pairs(0, pairs, last_step)
    finish(dp_copies)
    gain_total = gain_dp[0]
    for row in range(1, dp_count):
        gain_total = gain_total + gain_dp[row]
    gain_out_ref[...] = gain_total / math.sqrt(tokens)


def body(query_in, key_in, value_in, out_grad, log_decay, doc_ids, norm_gain):
    _, length, width = query_in.shape
    ctx_count, dp_count = lax.axis_size("ctx"), lax.axis_size("dp")
    heads = log_decay.shape[2]
    pairs = heads // 2
    lanes = 128
    chunk = pairs * 64 // ctx_count
    tokens = dp_count * ctx_count * query_in.shape[0] * length
    flat = jax.ShapeDtypeStruct((length, width), BF16)
    vmem = pl.BlockSpec(memory_space=pltpu.VMEM)
    wide, narrow = pltpu.VMEM((length, width), F32), pltpu.VMEM((length, width), BF16)
    whole_state = pltpu.VMEM((pairs * 64, lanes), BF16)
    pieces = pltpu.VMEM((ctx_count, chunk, lanes), BF16)
    dq, dk, dv, gain_grad = pl.pallas_call(
        functools.partial(kernel, ctx_count, dp_count, tokens),
        out_shape=(flat, flat, flat, jax.ShapeDtypeStruct((1, width), F32)),
        in_specs=[vmem] * 5 + [pl.BlockSpec(memory_space=pltpu.SMEM), vmem],
        out_specs=(vmem,) * 4,
        scratch_shapes=[
            pltpu.VMEM((heads, length), F32),
            pltpu.VMEM((pairs, length, 2 * length), F32),
            wide,
            wide,
            pltpu.VMEM((pairs, length, 2 * length), BF16),
            wide,
            narrow,
            narrow,
            wide,
            wide,
            pltpu.VMEM((ctx_count, pairs, lanes), F32),
            whole_state,
            pieces,
            pieces,
            whole_state,
            whole_state,
            pieces,
            pieces,
            whole_state,
            pltpu.VMEM((ctx_count, 1, width), F32),
            pltpu.VMEM((1, width), F32),
            pltpu.VMEM((dp_count, 1, width), F32),
            pltpu.SemaphoreType.DMA((6, ctx_count)),
            pltpu.SemaphoreType.DMA((6, ctx_count)),
            pltpu.SemaphoreType.DMA((dp_count,)),
            pltpu.SemaphoreType.DMA((dp_count,)),
        ],
        compiler_params=pltpu.CompilerParams(
            collective_id=0, has_side_effects=True, vmem_limit_bytes=40 * 1024 * 1024
        ),
    )(
        query_in[0], key_in[0], value_in[0], out_grad[0], log_decay[0], doc_ids,
        norm_gain.reshape(1, width),
    )
    return dq[None], dk[None], dv[None], gain_grad[0]


def solution(mesh):
    seq = P("dp", "ctx", None)
    return jax.shard_map(
        body,
        mesh=mesh,
        in_specs=(seq, seq, seq, seq, seq, P("dp", None), P()),
        out_specs=(seq, seq, seq, P()),
        check_vma=False,
    )
```

```python
import functools
import math

import jax
import jax.numpy as jnp
from jax import lax
from jax.experimental import pallas as pl
from jax.experimental.pallas import tpu as pltpu
from jax.sharding import PartitionSpec as P

EPSILON = 1e-05
MESH = pl.DeviceIdType.MESH
UNROLL = 8
F32 = jnp.float32
BF16 = jnp.bfloat16


def dot(left, right, left_dim, right_dim):
    return lax.dot_general(
        left, right, (((left_dim,), (right_dim,)), ((), ())), preferred_element_type=F32
    )


def kernel(
    ctx_count, dp_count, tokens,
    q_hbm, k_hbm, v_hbm, g_hbm, decay_hbm, doc_ref, gain_hbm,
    dq_ref, dk_ref, dv_ref, gain_out_ref,
    rows_s, weight_s, head_s, tail_s, probs_s, attn_s, grad_s, qw_s, dk_s, dv_s,
    carry_all, term_out, term_in, state_out, state_in,
    back_term_out, back_term_in, back_out, back_in,
    gain_out, gain_in, gain_sum, gain_rows, gain_full,
    q_ref, k_ref, v_ref, g_ref, decay_ref, gain_ref,
    send_sem, recv_sem, dp_send_sem, dp_recv_sem, load_sem,
):
    length, width = q_hbm.shape
    lanes = 128
    half = lanes // 2
    pairs = width // lanes
    chunk = pairs * half // ctx_count
    me = lax.axis_index("ctx")
    row_me = lax.axis_index("dp")

    loads = [
        pltpu.make_async_copy(source, target, load_sem.at[i])
        for i, (source, target) in enumerate(
            (
                (decay_hbm, decay_ref),
                (k_hbm, k_ref),
                (v_hbm, v_ref),
                (q_hbm, q_ref),
                (gain_hbm, gain_ref),
                (g_hbm, g_ref),
            )
        )
    ]
    for load in loads:
        load.start()

    barrier = pltpu.get_barrier_semaphore()
    for j in range(1, ctx_count):
        other = lax.rem(me + j, ctx_count)
        pl.semaphore_signal(barrier, inc=1, device_id={"ctx": other}, device_id_type=MESH)
    for j in range(1, dp_count):
        other = lax.rem(row_me + j, dp_count)
        pl.semaphore_signal(barrier, inc=1, device_id={"dp": other}, device_id_type=MESH)

    left_half = lax.broadcasted_iota(jnp.int32, (1, lanes), 1) < half

    def cols(pair):
        return pl.ds(pl.multiple_of(pair * lanes, lanes), lanes)

    def packed_rows(pair):
        return pl.ds(pl.multiple_of(pair * half, half), half)

    def pick(first, second):
        return jnp.where(left_half, first, second)

    def stacked(block):
        zero = jnp.zeros_like(block)
        return jnp.concatenate([pick(block, zero), pick(zero, block)], axis=0)

    def packed(full, size):
        return pick(full[:size], full[size:])

    def over_pairs(first, last, fn, init=0):
        return lax.fori_loop(first, last, fn, init, unroll=UNROLL)

    step_row = lax.broadcasted_iota(jnp.int32, (length, length), 0)
    step_col = lax.broadcasted_iota(jnp.int32, (length, length), 1)
    upto = jnp.where(step_row <= step_col, 1.0, 0.0).astype(BF16)
    loads[0].wait()
    rows_s[...] = dot(decay_ref[...], upto, 1, 0)
    loads[1].wait()
    loads[2].wait()

    same_doc = doc_ref[0, me] == doc_ref[0, jnp.maximum(me - 1, 0)]
    keep = jnp.where(same_doc, 1.0, 0.0) * jnp.where(me == 0, 0.0, 1.0)

    def column(head):
        row = rows_s[pl.ds(head, 1), :]
        return row, jnp.transpose(jnp.broadcast_to(row, (length, lanes)))

    def terms_step(pair, _):
        _, first = column(2 * pair)
        _, second = column(2 * pair + 1)
        within = pick(first, second)
        total = within[length - 1 :, :]
        tail = jnp.exp(total - within)
        tail_s[:, cols(pair)] = tail
        head_s[:, cols(pair)] = jnp.exp(within) * keep
        carry_all[me, pl.ds(pair, 1), :] = jnp.exp(total) * keep
        keyed = (k_ref[:, cols(pair)].astype(F32) * tail).astype(BF16)
        full = dot(keyed, v_ref[:, cols(pair)], 0, 0)
        term_out[packed_rows(pair), :] = packed(full, half).astype(BF16)
        return 0

    over_pairs(0, pairs, terms_step)
    pl.semaphore_wait(barrier, ctx_count - 1 + dp_count - 1)

    def piece(index):
        return pl.ds(pl.multiple_of(index * chunk, chunk), chunk)

    def to_all(phase, source, target):
        copies = []
        for j in range(1, ctx_count):
            other = lax.rem(me + j, ctx_count)
            copies.append(
                pltpu.make_async_remote_copy(
                    src_ref=source(other),
                    dst_ref=target(other),
                    send_sem=send_sem.at[phase, j],
                    recv_sem=recv_sem.at[phase, j],
                    device_id={"ctx": other},
                    device_id_type=MESH,
                )
            )
        for copy in copies:
            copy.start()
        return copies

    def finish(copies):
        for copy in copies:
            copy.wait()

    def combine(term_ref, out_ref, backward):
        per = max(chunk // half, 1)
        size = min(chunk, half)
        running = [jnp.zeros((size, lanes), F32) for _ in range(per)]
        order = range(ctx_count - 1, -1, -1) if backward else range(ctx_count)
        for block in order:
            for i in range(per):
                pair = lax.div(me * chunk, half) + i
                out_ref[block, i * size : (i + 1) * size, :] = running[i].astype(BF16)
                carry = carry_all[block, pl.ds(pair, 1), :]
                running[i] = carry * running[i] + term_ref[
                    block, i * size : (i + 1) * size, :
                ].astype(F32)

    def exchange_terms(phase, out_ref, in_ref):
        in_ref[me] = out_ref[piece(me), :]
        return to_all(phase, lambda other: out_ref.at[piece(other), :], lambda other: in_ref.at[me])

    def exchange_states(phase, out_ref, in_ref):
        in_ref[piece(me), :] = out_ref[me]
        return to_all(phase, lambda other: out_ref.at[other], lambda other: in_ref.at[piece(me), :])

    owned = max(chunk // half, 1)

    def owner_pairs(index):
        return pl.ds(lax.div(index * chunk, half), owned)

    carry_copies = to_all(
        0,
        lambda other: carry_all.at[me, owner_pairs(other), :],
        lambda other: carry_all.at[me, owner_pairs(other), :],
    )
    term_copies = exchange_terms(1, term_out, term_in)

    causal = step_row >= step_col

    def local_step(pair, _):
        weights = []
        for head in (2 * pair, 2 * pair + 1):
            row, col = column(head)
            weights.append(jnp.where(causal, jnp.exp(jnp.minimum(col - row, 0.0)), 0.0))
        weight = jnp.concatenate(weights, axis=1)
        weight_s[pair] = weight
        scores = dot(q_ref[:, cols(pair)], stacked(k_ref[:, cols(pair)]), 1, 1)
        probs = (scores * weight).astype(BF16)
        probs_s[pair] = probs
        attn_s[:, cols(pair)] = dot(probs, stacked(v_ref[:, cols(pair)]), 1, 0)
        qw_s[:, cols(pair)] = (q_ref[:, cols(pair)].astype(F32) * head_s[:, cols(pair)]).astype(BF16)
        return 0

    loads[3].wait()
    over_pairs(0, pairs // 2, local_step)
    finish(carry_copies)
    finish(term_copies)
    combine(term_in, state_out, False)
    state_copies = exchange_states(2, state_out, state_in)
    over_pairs(pairs // 2, pairs, local_step)
    finish(state_copies)

    def attend_step(pair, sums):
        square, cross = sums
        carried = dot(qw_s[:, cols(pair)], stacked(state_in[packed_rows(pair), :]), 1, 0)
        attn = attn_s[:, cols(pair)] + carried
        attn_s[:, cols(pair)] = attn
        scaled = gain_ref[:, cols(pair)] * g_ref[:, cols(pair)].astype(F32)
        return square + attn * attn, cross + attn * scaled

    loads[4].wait()
    loads[5].wait()
    zero = jnp.zeros((length, lanes), F32)
    square, cross = over_pairs(0, pairs, attend_step, (zero, zero))
    inv_rms = lax.rsqrt(jnp.sum(square, axis=1, keepdims=True) / width + EPSILON)
    shift = inv_rms * inv_rms * inv_rms * jnp.sum(cross, axis=1, keepdims=True) / width

    share = width // ctx_count

    def norm_step(pair, _):
        grad_out = g_ref[:, cols(pair)].astype(F32)
        attn = attn_s[:, cols(pair)]
        grad = inv_rms * (gain_ref[:, cols(pair)] * grad_out) - shift * attn
        grad = grad.astype(BF16)
        grad_s[:, cols(pair)] = grad
        full = dot(qw_s[:, cols(pair)], grad, 0, 0)
        back_term_out[packed_rows(pair), :] = packed(full, half).astype(BF16)
        gain_row = jnp.sum(grad_out * attn * inv_rms, axis=0, keepdims=True)
        if share < lanes:
            for i in range(lanes // share):
                gain_out[pair * (lanes // share) + i] = gain_row[:, i * share : (i + 1) * share]
        else:
            per = share // lanes
            gain_out[lax.div(pair, per), :, cols(lax.rem(pair, per))] = gain_row
        return 0

    over_pairs(0, pairs, norm_step)
    gain_in[me] = gain_out[me]
    gain_copies = to_all(5, lambda other: gain_out.at[other], lambda other: gain_in.at[me])
    back_term_copies = exchange_terms(3, back_term_out, back_term_in)

    def grads_step(pair, _):
        grad = grad_s[:, cols(pair)]
        scores = dot(grad, stacked(v_ref[:, cols(pair)]), 1, 1)
        scores = (scores * weight_s[pair]).astype(BF16)
        weighted = (grad.astype(F32) * head_s[:, cols(pair)]).astype(BF16)
        dq = dot(scores, stacked(k_ref[:, cols(pair)]), 1, 0)
        dq = dq + dot(weighted, stacked(state_in[packed_rows(pair), :]), 1, 1)
        dq_ref[:, cols(pair)] = dq.astype(BF16)
        dk_s[:, cols(pair)] = packed(dot(scores, q_ref[:, cols(pair)], 0, 0), length)
        dv_s[:, cols(pair)] = packed(dot(probs_s[pair], grad, 0, 0), length)
        return 0

    over_pairs(0, pairs // 2, grads_step)
    finish(gain_copies)
    total = gain_in[0]
    for block in range(1, ctx_count):
        total = total + gain_in[block]
    gain_rows[row_me] = total
    dp_copies = []
    for j in range(1, dp_count):
        other = lax.rem(row_me + j, dp_count)
        dp_copies.append(
            pltpu.make_async_remote_copy(
                src_ref=gain_rows.at[row_me],
                dst_ref=gain_rows.at[row_me],
                send_sem=dp_send_sem.at[j],
                recv_sem=dp_recv_sem.at[j],
                device_id={"dp": other},
                device_id_type=MESH,
            )
        )
    for copy in dp_copies:
        copy.start()
    finish(back_term_copies)
    combine(back_term_in, back_out, True)
    back_copies = exchange_states(4, back_out, back_in)
    over_pairs(pairs // 2, pairs, grads_step)
    finish(dp_copies)
    total = gain_rows[0]
    for row in range(1, dp_count):
        total = total + gain_rows[row]
    total = total / math.sqrt(tokens)
    gain_sum[...] = total
    gain_full[me] = total
    full_copies = to_all(6, lambda other: gain_sum, lambda other: gain_full.at[me])
    finish(back_copies)

    def last_step(pair, _):
        back = stacked(back_in[packed_rows(pair), :])
        tail = tail_s[:, cols(pair)]
        dk = dk_s[:, cols(pair)] + tail * dot(v_ref[:, cols(pair)], back, 1, 1)
        dv = dv_s[:, cols(pair)] + tail * dot(k_ref[:, cols(pair)], back, 1, 0)
        dk_ref[:, cols(pair)] = dk.astype(BF16)
        dv_ref[:, cols(pair)] = dv.astype(BF16)
        return 0

    over_pairs(0, pairs, last_step)
    finish(full_copies)
    for block in range(ctx_count):
        gain_out_ref[:, block * share : (block + 1) * share] = gain_full[block]


def write_out(*refs):
    sources, targets, sem = refs[:4], refs[4:8], refs[8]
    copies = [
        pltpu.make_async_copy(source, target, sem.at[i])
        for i, (source, target) in enumerate(zip(sources, targets))
    ]
    for copy in copies:
        copy.start()
    for copy in copies:
        copy.wait()


def body(query_in, key_in, value_in, out_grad, log_decay, doc_ids, norm_gain):
    _, length, width = query_in.shape
    ctx_count, dp_count = lax.axis_size("ctx"), lax.axis_size("dp")
    heads = log_decay.shape[2]
    pairs = heads // 2
    lanes = 128
    chunk = pairs * 64 // ctx_count
    tokens = dp_count * ctx_count * query_in.shape[0] * length
    flat = jax.ShapeDtypeStruct((length, width), BF16)
    vmem = pl.BlockSpec(memory_space=pltpu.VMEM)
    wide, narrow = pltpu.VMEM((length, width), F32), pltpu.VMEM((length, width), BF16)
    whole_state = pltpu.VMEM((pairs * 64, lanes), BF16)
    pieces = pltpu.VMEM((ctx_count, chunk, lanes), BF16)
    anywhere = pl.BlockSpec(memory_space=pl.ANY)
    outs = (flat, flat, flat, jax.ShapeDtypeStruct((1, width), F32))
    gain_share = width // ctx_count
    gain_pieces = pltpu.VMEM((ctx_count, 1, gain_share), F32)
    results = pl.pallas_call(
        functools.partial(kernel, ctx_count, dp_count, tokens),
        out_shape=outs,
        in_specs=[anywhere] * 5 + [pl.BlockSpec(memory_space=pltpu.SMEM), anywhere],
        out_specs=(vmem,) * 4,
        scratch_shapes=[
            pltpu.VMEM((heads, length), F32),
            pltpu.VMEM((pairs, length, 2 * length), F32),
            wide,
            wide,
            pltpu.VMEM((pairs, length, 2 * length), BF16),
            wide,
            narrow,
            narrow,
            wide,
            wide,
            pltpu.VMEM((ctx_count, pairs, lanes), F32),
            whole_state,
            pieces,
            pieces,
            whole_state,
            whole_state,
            pieces,
            pieces,
            whole_state,
            gain_pieces,
            gain_pieces,
            pltpu.VMEM((1, gain_share), F32),
            pltpu.VMEM((dp_count, 1, gain_share), F32),
            gain_pieces,
            narrow,
            narrow,
            narrow,
            narrow,
            pltpu.VMEM((heads, length), BF16),
            pltpu.VMEM((1, width), F32),
            pltpu.SemaphoreType.DMA((7, ctx_count)),
            pltpu.SemaphoreType.DMA((7, ctx_count)),
            pltpu.SemaphoreType.DMA((dp_count,)),
            pltpu.SemaphoreType.DMA((dp_count,)),
            pltpu.SemaphoreType.DMA((6,)),
        ],
        compiler_params=pltpu.CompilerParams(
            collective_id=0, has_side_effects=True, vmem_limit_bytes=56 * 1024 * 1024
        ),
    )(
        query_in[0], key_in[0], value_in[0], out_grad[0], log_decay[0].T, doc_ids,
        norm_gain.reshape(1, width),
    )
    dq, dk, dv, gain_grad = pl.pallas_call(
        write_out,
        out_shape=outs,
        in_specs=[vmem] * 4,
        out_specs=(anywhere,) * 4,
        scratch_shapes=[pltpu.SemaphoreType.DMA((4,))],
        compiler_params=pltpu.CompilerParams(vmem_limit_bytes=56 * 1024 * 1024),
    )(*results)
    return dq[None], dk[None], dv[None], gain_grad[0]


def solution(mesh):
    seq = P("dp", "ctx", None)
    return jax.shard_map(
        body,
        mesh=mesh,
        in_specs=(seq, seq, seq, seq, seq, P("dp", None), P()),
        out_specs=(seq, seq, seq, P()),
        check_vma=False,
    )
```

```python
import functools
import math

import jax
import jax.numpy as jnp
from jax import lax
from jax.experimental import pallas as pl
from jax.experimental.pallas import tpu as pltpu
from jax.sharding import PartitionSpec as P

EPSILON = 1e-05
MESH = pl.DeviceIdType.MESH
UNROLL = 8
F32 = jnp.float32
BF16 = jnp.bfloat16


def dot(left, right, left_dim, right_dim):
    return lax.dot_general(
        left, right, (((left_dim,), (right_dim,)), ((), ())), preferred_element_type=F32
    )


def kernel(
    ctx_count, dp_count, tokens,
    q_hbm, k_hbm, v_hbm, g_hbm, decay_hbm, doc_ref, gain_hbm,
    dq_ref, dk_ref, dv_ref, gain_out_ref,
    rows_s, weight_s, head_s, tail_s, probs_s, attn_s, grad_s, qw_s, dk_s, dv_s,
    carry_all, term_out, term_in, state_out, state_in,
    back_term_out, back_term_in, back_out, back_in,
    gain_out, gain_in, gain_sum, gain_rows, gain_full,
    q_ref, k_ref, v_ref, g_ref, decay_ref, gain_ref,
    send_sem, recv_sem, dp_send_sem, dp_recv_sem, load_sem,
):
    length, width = q_hbm.shape
    lanes = 128
    half = lanes // 2
    pairs = width // lanes
    chunk = pairs * half // ctx_count
    me = lax.axis_index("ctx")
    row_me = lax.axis_index("dp")

    loads = [
        pltpu.make_async_copy(source, target, load_sem.at[i])
        for i, (source, target) in enumerate(
            (
                (decay_hbm, decay_ref),
                (k_hbm, k_ref),
                (v_hbm, v_ref),
                (q_hbm, q_ref),
                (gain_hbm, gain_ref),
                (g_hbm, g_ref),
            )
        )
    ]
    for load in loads:
        load.start()

    barrier = pltpu.get_barrier_semaphore()
    for j in range(1, ctx_count):
        other = lax.rem(me + j, ctx_count)
        pl.semaphore_signal(barrier, inc=1, device_id={"ctx": other}, device_id_type=MESH)
    for j in range(1, dp_count):
        other = lax.rem(row_me + j, dp_count)
        pl.semaphore_signal(barrier, inc=1, device_id={"dp": other}, device_id_type=MESH)

    left_half = lax.broadcasted_iota(jnp.int32, (1, lanes), 1) < half

    def cols(pair):
        return pl.ds(pl.multiple_of(pair * lanes, lanes), lanes)

    def packed_rows(pair):
        return pl.ds(pl.multiple_of(pair * half, half), half)

    def pick(first, second):
        return jnp.where(left_half, first, second)

    def stacked(block):
        zero = jnp.zeros_like(block)
        return jnp.concatenate([pick(block, zero), pick(zero, block)], axis=0)

    def packed(full, size):
        return pick(full[:size], full[size:])

    def over_pairs(first, last, fn, init=0):
        return lax.fori_loop(first, last, fn, init, unroll=UNROLL)

    step_row = lax.broadcasted_iota(jnp.int32, (length, length), 0)
    step_col = lax.broadcasted_iota(jnp.int32, (length, length), 1)
    upto = jnp.where(step_row <= step_col, 1.0, 0.0).astype(BF16)
    loads[0].wait()
    rows_s[...] = dot(decay_ref[...], upto, 1, 0)
    loads[1].wait()
    loads[2].wait()

    same_doc = doc_ref[0, me] == doc_ref[0, jnp.maximum(me - 1, 0)]
    keep = jnp.where(same_doc, 1.0, 0.0) * jnp.where(me == 0, 0.0, 1.0)

    def column(head):
        row = rows_s[pl.ds(head, 1), :]
        return row, jnp.transpose(jnp.broadcast_to(row, (length, lanes)))

    def terms_step(pair, _):
        _, first = column(2 * pair)
        _, second = column(2 * pair + 1)
        within = pick(first, second)
        total = within[length - 1 :, :]
        tail = jnp.exp(total - within)
        tail_s[:, cols(pair)] = tail
        head_s[:, cols(pair)] = jnp.exp(within) * keep
        carry_all[me, pl.ds(pair, 1), :] = jnp.exp(total) * keep
        keyed = (k_ref[:, cols(pair)].astype(F32) * tail).astype(BF16)
        full = dot(keyed, v_ref[:, cols(pair)], 0, 0)
        term_out[packed_rows(pair), :] = packed(full, half).astype(BF16)
        return 0

    over_pairs(0, pairs, terms_step)
    pl.semaphore_wait(barrier, ctx_count - 1 + dp_count - 1)

    def piece(index):
        return pl.ds(pl.multiple_of(index * chunk, chunk), chunk)

    def to_all(phase, source, target):
        copies = []
        for j in range(1, ctx_count):
            other = lax.rem(me + j, ctx_count)
            copies.append(
                pltpu.make_async_remote_copy(
                    src_ref=source(other),
                    dst_ref=target(other),
                    send_sem=send_sem.at[phase, j],
                    recv_sem=recv_sem.at[phase, j],
                    device_id={"ctx": other},
                    device_id_type=MESH,
                )
            )
        for copy in copies:
            copy.start()
        return copies

    def finish(copies):
        for copy in copies:
            copy.wait()

    def combine(term_ref, out_ref, backward):
        per = max(chunk // half, 1)
        size = min(chunk, half)
        running = [jnp.zeros((size, lanes), F32) for _ in range(per)]
        order = range(ctx_count - 1, -1, -1) if backward else range(ctx_count)
        for block in order:
            for i in range(per):
                pair = lax.div(me * chunk, half) + i
                out_ref[block, i * size : (i + 1) * size, :] = running[i].astype(BF16)
                carry = carry_all[block, pl.ds(pair, 1), :]
                running[i] = carry * running[i] + term_ref[
                    block, i * size : (i + 1) * size, :
                ].astype(F32)

    def exchange_terms(phase, out_ref, in_ref):
        in_ref[me] = out_ref[piece(me), :]
        return to_all(phase, lambda other: out_ref.at[piece(other), :], lambda other: in_ref.at[me])

    def exchange_states(phase, out_ref, in_ref):
        in_ref[piece(me), :] = out_ref[me]
        return to_all(phase, lambda other: out_ref.at[other], lambda other: in_ref.at[piece(me), :])

    owned = max(chunk // half, 1)

    def owner_pairs(index):
        return pl.ds(lax.div(index * chunk, half), owned)

    carry_copies = to_all(
        0,
        lambda other: carry_all.at[me, owner_pairs(other), :],
        lambda other: carry_all.at[me, owner_pairs(other), :],
    )
    term_copies = exchange_terms(1, term_out, term_in)

    causal = step_row >= step_col

    def local_step(pair, _):
        weights = []
        for head in (2 * pair, 2 * pair + 1):
            row, col = column(head)
            weights.append(jnp.where(causal, jnp.exp(jnp.minimum(col - row, 0.0)), 0.0))
        weight = jnp.concatenate(weights, axis=1)
        weight_s[pair] = weight
        scores = dot(q_ref[:, cols(pair)], stacked(k_ref[:, cols(pair)]), 1, 1)
        probs = (scores * weight).astype(BF16)
        probs_s[pair] = probs
        attn_s[:, cols(pair)] = dot(probs, stacked(v_ref[:, cols(pair)]), 1, 0)
        qw_s[:, cols(pair)] = (q_ref[:, cols(pair)].astype(F32) * head_s[:, cols(pair)]).astype(BF16)
        return 0

    loads[3].wait()
    over_pairs(0, pairs // 2, local_step)
    finish(carry_copies)
    finish(term_copies)
    combine(term_in, state_out, False)
    state_copies = exchange_states(2, state_out, state_in)
    over_pairs(pairs // 2, pairs, local_step)
    finish(state_copies)

    def attend_step(pair, sums):
        square, cross = sums
        carried = dot(qw_s[:, cols(pair)], stacked(state_in[packed_rows(pair), :]), 1, 0)
        attn = attn_s[:, cols(pair)] + carried
        attn_s[:, cols(pair)] = attn
        scaled = gain_ref[:, cols(pair)] * g_ref[:, cols(pair)].astype(F32)
        return square + attn * attn, cross + attn * scaled

    loads[4].wait()
    loads[5].wait()
    zero = jnp.zeros((length, lanes), F32)
    square, cross = over_pairs(0, pairs, attend_step, (zero, zero))
    inv_rms = lax.rsqrt(jnp.sum(square, axis=1, keepdims=True) / width + EPSILON)
    shift = inv_rms * inv_rms * inv_rms * jnp.sum(cross, axis=1, keepdims=True) / width

    share = width // ctx_count

    def norm_step(pair, _):
        grad_out = g_ref[:, cols(pair)].astype(F32)
        attn = attn_s[:, cols(pair)]
        grad = inv_rms * (gain_ref[:, cols(pair)] * grad_out) - shift * attn
        grad = grad.astype(BF16)
        grad_s[:, cols(pair)] = grad
        full = dot(qw_s[:, cols(pair)], grad, 0, 0)
        back_term_out[packed_rows(pair), :] = packed(full, half).astype(BF16)
        gain_row = jnp.sum(grad_out * attn * inv_rms, axis=0, keepdims=True)
        if share < lanes:
            for i in range(lanes // share):
                gain_out[pair * (lanes // share) + i] = gain_row[:, i * share : (i + 1) * share]
        else:
            per = share // lanes
            gain_out[lax.div(pair, per), :, cols(lax.rem(pair, per))] = gain_row
        return 0

    over_pairs(0, pairs, norm_step)
    gain_in[me] = gain_out[me]
    gain_copies = to_all(5, lambda other: gain_out.at[other], lambda other: gain_in.at[me])
    back_term_copies = exchange_terms(3, back_term_out, back_term_in)

    def grads_step(pair, _):
        grad = grad_s[:, cols(pair)]
        scores = dot(grad, stacked(v_ref[:, cols(pair)]), 1, 1)
        scores = (scores * weight_s[pair]).astype(BF16)
        weighted = (grad.astype(F32) * head_s[:, cols(pair)]).astype(BF16)
        dq = dot(scores, stacked(k_ref[:, cols(pair)]), 1, 0)
        dq = dq + dot(weighted, stacked(state_in[packed_rows(pair), :]), 1, 1)
        dq_ref[:, cols(pair)] = dq.astype(BF16)
        dk_s[:, cols(pair)] = packed(dot(scores, q_ref[:, cols(pair)], 0, 0), length)
        dv_s[:, cols(pair)] = packed(dot(probs_s[pair], grad, 0, 0), length)
        return 0

    over_pairs(0, pairs // 2, grads_step)
    finish(gain_copies)
    total = gain_in[0]
    for block in range(1, ctx_count):
        total = total + gain_in[block]
    gain_rows[row_me] = total
    dp_copies = []
    for j in range(1, dp_count):
        other = lax.rem(row_me + j, dp_count)
        dp_copies.append(
            pltpu.make_async_remote_copy(
                src_ref=gain_rows.at[row_me],
                dst_ref=gain_rows.at[row_me],
                send_sem=dp_send_sem.at[j],
                recv_sem=dp_recv_sem.at[j],
                device_id={"dp": other},
                device_id_type=MESH,
            )
        )
    for copy in dp_copies:
        copy.start()
    finish(back_term_copies)
    combine(back_term_in, back_out, True)
    back_copies = exchange_states(4, back_out, back_in)
    over_pairs(pairs // 2, pairs, grads_step)
    finish(dp_copies)
    total = gain_rows[0]
    for row in range(1, dp_count):
        total = total + gain_rows[row]
    total = total / math.sqrt(tokens)
    gain_sum[...] = total
    gain_full[me] = total
    full_copies = to_all(6, lambda other: gain_sum, lambda other: gain_full.at[me])
    finish(back_copies)

    def last_step(pair, _):
        back = stacked(back_in[packed_rows(pair), :])
        tail = tail_s[:, cols(pair)]
        dk = dk_s[:, cols(pair)] + tail * dot(v_ref[:, cols(pair)], back, 1, 1)
        dv = dv_s[:, cols(pair)] + tail * dot(k_ref[:, cols(pair)], back, 1, 0)
        dk_ref[:, cols(pair)] = dk.astype(BF16)
        dv_ref[:, cols(pair)] = dv.astype(BF16)
        return 0

    over_pairs(0, pairs, last_step)
    finish(full_copies)
    for block in range(ctx_count):
        gain_out_ref[:, block * share : (block + 1) * share] = gain_full[block]


def write_out(*refs):
    sources, targets, staged, in_sem, out_sem = refs[:4], refs[4:8], refs[8:12], refs[12], refs[13]
    moves = []
    for source, target, stage in zip(sources, targets, staged):
        count = source.shape[0]
        step = max(count // 2, 1)
        for first in range(0, count, step):
            rows, i = pl.ds(first, step), len(moves)
            moves.append(
                (
                    pltpu.make_async_copy(source.at[rows, :], stage.at[rows, :], in_sem.at[i]),
                    pltpu.make_async_copy(stage.at[rows, :], target.at[rows, :], out_sem.at[i]),
                )
            )
    for load, _ in moves:
        load.start()
    for load, store in moves:
        load.wait()
        store.start()
    for _, store in moves:
        store.wait()


def body(query_in, key_in, value_in, out_grad, log_decay, doc_ids, norm_gain):
    _, length, width = query_in.shape
    ctx_count, dp_count = lax.axis_size("ctx"), lax.axis_size("dp")
    heads = log_decay.shape[2]
    pairs = heads // 2
    lanes = 128
    chunk = pairs * 64 // ctx_count
    tokens = dp_count * ctx_count * query_in.shape[0] * length
    flat = jax.ShapeDtypeStruct((length, width), BF16)
    vmem = pl.BlockSpec(memory_space=pltpu.VMEM)
    wide, narrow = pltpu.VMEM((length, width), F32), pltpu.VMEM((length, width), BF16)
    whole_state = pltpu.VMEM((pairs * 64, lanes), BF16)
    pieces = pltpu.VMEM((ctx_count, chunk, lanes), BF16)
    anywhere = pl.BlockSpec(memory_space=pl.ANY)
    outs = (flat, flat, flat, jax.ShapeDtypeStruct((1, width), F32))
    gain_share = width // ctx_count
    gain_pieces = pltpu.VMEM((ctx_count, 1, gain_share), F32)
    results = pl.pallas_call(
        functools.partial(kernel, ctx_count, dp_count, tokens),
        out_shape=outs,
        in_specs=[anywhere] * 5 + [pl.BlockSpec(memory_space=pltpu.SMEM), anywhere],
        out_specs=(vmem,) * 4,
        scratch_shapes=[
            pltpu.VMEM((heads, length), F32),
            pltpu.VMEM((pairs, length, 2 * length), F32),
            wide,
            wide,
            pltpu.VMEM((pairs, length, 2 * length), BF16),
            wide,
            narrow,
            narrow,
            wide,
            wide,
            pltpu.VMEM((ctx_count, pairs, lanes), F32),
            whole_state,
            pieces,
            pieces,
            whole_state,
            whole_state,
            pieces,
            pieces,
            whole_state,
            gain_pieces,
            gain_pieces,
            pltpu.VMEM((1, gain_share), F32),
            pltpu.VMEM((dp_count, 1, gain_share), F32),
            gain_pieces,
            narrow,
            narrow,
            narrow,
            narrow,
            pltpu.VMEM((heads, length), BF16),
            pltpu.VMEM((1, width), F32),
            pltpu.SemaphoreType.DMA((7, ctx_count)),
            pltpu.SemaphoreType.DMA((7, ctx_count)),
            pltpu.SemaphoreType.DMA((dp_count,)),
            pltpu.SemaphoreType.DMA((dp_count,)),
            pltpu.SemaphoreType.DMA((6,)),
        ],
        compiler_params=pltpu.CompilerParams(
            collective_id=0, has_side_effects=True, vmem_limit_bytes=56 * 1024 * 1024
        ),
    )(
        query_in[0], key_in[0], value_in[0], out_grad[0], log_decay[0].T, doc_ids,
        norm_gain.reshape(1, width),
    )
    dq, dk, dv, gain_grad = pl.pallas_call(
        write_out,
        out_shape=outs,
        in_specs=[anywhere] * 4,
        out_specs=(anywhere,) * 4,
        scratch_shapes=[narrow] * 3
        + [pltpu.VMEM((1, width), F32)]
        + [pltpu.SemaphoreType.DMA((7,))] * 2,
        compiler_params=pltpu.CompilerParams(vmem_limit_bytes=56 * 1024 * 1024),
    )(*results)
    return dq[None], dk[None], dv[None], gain_grad[0]


def solution(mesh):
    seq = P("dp", "ctx", None)
    return jax.shard_map(
        body,
        mesh=mesh,
        in_specs=(seq, seq, seq, seq, seq, P("dp", None), P()),
        out_specs=(seq, seq, seq, P()),
        check_vma=False,
    )
```
